32 devices in a mesh: groups: 2 (over x), block: 16 (over z, y, core).
Axes of the slice: x: 2, y: 2, z: 4, core: 2. Of those that a mesh axis runs over, the one named last changes fastest.
Arguments:
- inflow: bfloat16 [4, 256, 16, 256], P(None, ('groups', 'block')), parts along dimension 1, may hold values from -6 to 6
- speed_bin: int32 [2], P('groups'), parts along dimension 0, may hold values from 0 to 15
- bin_table: bfloat16 [16, 32], replicated, may hold values from -3 to 3
- w_in: bfloat16 [3, 3, 3, 32, 4], replicated, may hold values from -0.625 to 0.625
- w_mid: bfloat16 [3, 3, 3, 64, 32], replicated, may hold values from -0.3125 to 0.3125
- w_dec: bfloat16 [3, 3, 3, 32, 96], replicated, may hold values from -0.15625 to 0.15625
- w_out: bfloat16 [4, 32], replicated, may hold values from -1.5 to 1.5
- grad_pred: bfloat16 [4, 256, 16, 256], P(None, ('groups', 'block')), parts along dimension 1, may hold values from -0.0059814453 to 0.0059814453
Outputs:
- pred: float32 [4, 256, 16, 256], P(None, ('groups', 'block')), parts along dimension 1
- grad_w_out: float32 [8, 32], P('groups'), parts along dimension 0
- grad_w_dec: float32 [6, 3, 3, 32, 96], P('groups'), parts along dimension 0
- grad_w_mid: float32 [6, 3, 3, 64, 32], P('groups'), parts along dimension 0
The draws below stay inside these ranges and needn't reach their ends.
There are 2 independent parts, one for each index of `groups`. The reference program is written for one: setup_inputs(seed, part) draws one part's arguments, and reference() takes and returns one part's arrays. A program takes and returns all parts, laid end to end along the dimension named above; an argument that names none is the same for every part. Nothing has to cross between parts.
All inputs are finite; a program needn't handle non-finite values.
Results may differ from the reference program's by a relative error of at most 0.015.
Values may be sent and summed in bfloat16 or wider, within the bound.
A program may use at most 448 MiB of HBM per device.

```python
import jax
import jax.numpy as jnp
from jax import lax

CIN = 4
COUT = 4
C1 = 32
C2 = 64
NBINS = 16
NY = 16
NZ = 256
NX = 128


def block_levels(key, shape, split, low, high):
    level = 1.0
    for position, parts in split:
        heights = jax.random.uniform(jax.random.fold_in(jax.random.fold_in(key, 6), position), (parts,), jnp.float32, low / len(split), high / len(split))
        level = level * jnp.repeat(jnp.exp(heights), shape[position] // parts).reshape((-1,) + (1,) * (len(shape) - 1 - position))
    return level


def noise(rng, shape, deviation, bound, shards=(), held_as=jnp.bfloat16):
    entries = jax.random.normal(rng, shape, jnp.float32) * deviation
    if len(shards) > 0:
        entries = block_levels(rng, shape, shards, -0.22, 0.18) * entries
    return jnp.clip(entries, min=-bound, max=bound).astype(held_as)


def setup_inputs(seed: int = 0, part: int = 0) -> dict:
    splits = jax.random.split(jax.random.key(seed), 9)
    part_splits = jax.random.split(jax.random.fold_in(splits[8], part), 9)
    return {
        "inflow": noise(part_splits[0], (CIN, NX, NY, NZ), 1.0, 6.0, ((1, 16),)),
        "speed_bin": jax.random.randint(part_splits[1], (1,), 0, NBINS).astype(jnp.int32),
        "bin_table": noise(splits[2], (NBINS, C1), 0.5, 3.0),
        "w_in": noise(splits[3], (3, 3, 3, C1, CIN), (27 * CIN) ** -0.5, 0.625),
        "w_mid": noise(splits[4], (3, 3, 3, C2, C1), (27 * C1 // 2) ** -0.5, 0.3125),
        "w_dec": noise(splits[5], (3, 3, 3, C1, C2 + C1), (27 * (C2 + C1) // 2) ** -0.5, 0.15625),
        "w_out": noise(splits[6], (COUT, C1), (C1 // 2) ** -0.5, 1.5),
        "grad_pred": noise(part_splits[7], (COUT, NX, NY, NZ), 0.001, 0.0059814453, ((1, 16),)),
    }


def conv(field, kernel):
    return lax.conv_general_dilated(field[None], kernel, (1, 1, 1), 'SAME', dimension_numbers=('NCDHW', 'DHWOI', 'NCDHW'), precision=lax.Precision.HIGHEST)[0]

def pool_sum(field):
    chans, sx, sy, sz = field.shape
    return field.reshape(chans, sx // 2, 2, sy // 2, 2, sz // 2, 2).sum(axis=(2, 4, 6))

def upsample(field):
    return jnp.repeat(jnp.repeat(jnp.repeat(field, 2, axis=1), 2, axis=2), 2, axis=3)

def silu_slope(value):
    sig = jax.nn.sigmoid(value)
    return sig * (1.0 + value * (1.0 - sig))

def reference(inflow, speed_bin, bin_table, w_in, w_mid, w_dec, w_out, grad_pred):
    table = bin_table.astype(jnp.float32)
    onehot = (jnp.arange(NBINS, dtype=jnp.int32) == speed_bin[0]).astype(jnp.float32)
    bias = jnp.dot(onehot, table, precision=lax.Precision.HIGHEST)
    enc = jax.nn.relu(conv(inflow.astype(jnp.float32), w_in.astype(jnp.float32)) + bias[:, None, None, None]).astype(jnp.bfloat16)
    pooled = (pool_sum(enc.astype(jnp.float32)) * 0.125).astype(jnp.bfloat16)
    coarse_pre = conv(pooled.astype(jnp.float32), w_mid.astype(jnp.float32))
    coarse = jax.nn.silu(coarse_pre).astype(jnp.bfloat16)
    joined = jnp.concatenate([upsample(coarse), enc], axis=0)
    dec_pre = conv(joined.astype(jnp.float32), w_dec.astype(jnp.float32))
    dec = jax.nn.silu(dec_pre).astype(jnp.bfloat16)
    dec_f = dec.astype(jnp.float32)
    out_f = w_out.astype(jnp.float32)
    grad_f = grad_pred.astype(jnp.float32)
    pred = jnp.einsum('oc,cxyz->oxyz', out_f, dec_f, precision=lax.Precision.HIGHEST)
    grad_w_out = jnp.einsum('oxyz,cxyz->oc', grad_f, dec_f, precision=lax.Precision.HIGHEST)
    back = jnp.einsum('oc,oxyz->cxyz', out_f, grad_f, precision=lax.Precision.HIGHEST)
    grad_dec = (back * silu_slope(dec_pre)).astype(jnp.bfloat16)
    outputs, pullback = jax.vjp(conv, joined.astype(jnp.float32), w_dec.astype(jnp.float32))
    grad_joined, grad_w_dec = pullback(grad_dec.astype(outputs.dtype))
    grad_up = grad_joined[:C2]
    pooled_up = pool_sum(grad_up)
    grad_coarse = (pooled_up * silu_slope(coarse_pre)).astype(jnp.bfloat16)
    mid_out, mid_pull = jax.vjp(conv, pooled.astype(jnp.float32), w_mid.astype(jnp.float32))
    unused, grad_w_mid = mid_pull(grad_coarse.astype(mid_out.dtype))
    return (pred, grad_w_out, grad_w_dec, grad_w_mid)
```

```python
import jax
import jax.numpy as jnp
import numpy as np
from jax import lax
from jax.experimental import pallas as pl
from jax.experimental.pallas import tpu as pltpu
from jax.sharding import PartitionSpec as P

F32, BF16 = jnp.float32, jnp.bfloat16
LANES = 128
YC = 8
CELLS = YC * LANES
WIDE = CELLS + 2 * LANES
WINDOW = ((1, 0), (0, LANES), (1, LANES), (0, 2 * LANES))
PARITIES = tuple((p // 4, p // 2 % 2, p % 2) for p in range(8))


def place_tables():
    fine = np.zeros((2, 3, 4), np.float32)
    coarse = np.zeros((2, 3, 3), np.float32)
    child = np.zeros((3, 4), np.float32)
    for p in range(2):
        for a in range(3):
            fine[p, a, p + a] = 1
            coarse[p, a, (p + a - 1) // 2 + 1] = 1
            child[a, p + 2 - a] += 1
    t_in = np.einsum("pax,qby,rez->pqrabexzy", fine, fine, fine).reshape(8, 27, 64)
    t_skip = np.einsum("pax,qby,rez->pqrabeyxz", fine, fine, fine).reshape(8, 27, 64)
    t_up = np.einsum("pax,qby,rez->pqrabeyxz", coarse, coarse, coarse).reshape(8, 27, 27)
    t_adj = np.einsum("ax,by,ez->abeyxz", child, child, child).reshape(27, 64)
    order = np.zeros((8, 8), np.float32)
    for i, (px, py, pz) in enumerate(PARITIES):
        order[i, px * 4 + pz * 2 + py] = 1
    split = np.zeros((256, 512), np.float32)
    merge = np.zeros((256, 256), np.float32)
    for z in range(LANES):
        for w in range(4):
            if 0 <= 2 * z - 1 + w < 256:
                split[2 * z - 1 + w, w * LANES + z] = 1
        for p in range(2):
            merge[p * LANES + z, 2 * z + p] = 1
    return t_in, t_skip, t_up, t_adj, order, split, merge


def dot(a, b):
    return jnp.dot(a, b, preferred_element_type=F32)


def shifted(v, by):
    z = lax.broadcasted_iota(jnp.int32, v.shape, 1) % LANES
    if by == 1:
        return jnp.where(z == 0, 0.0, pltpu.roll(v, 1, 1))
    return jnp.where(z == LANES - 1, 0.0, pltpu.roll(v, v.shape[1] - 1, 1))


def row(start, size, unit):
    return pl.ds(pl.multiple_of(start * unit, unit), size)


def put_fine(ref, par, line, low, high):
    block = jnp.concatenate([shifted(high, 1), low, high, shifted(low, -1)], axis=0)
    ref[par, row(line, 128, 128), LANES : LANES + CELLS] = block.astype(BF16)


def put_coarse(ref, plane, v):
    block = jnp.concatenate([shifted(v, 1), v, shifted(v, -1)], axis=0)
    n = 3 * v.shape[0]
    ref[row(plane, n, n), LANES : LANES + CELLS] = block.astype(BF16)


def rows_to_lanes(v, first, count, lane):
    return jnp.concatenate(
        [v[8 * y + first : 8 * y + first + count, lane : lane + LANES] for y in range(YC)], axis=1
    )


def body(
    edge, before, inflow, after, gp, bias, w_in, w_mid, w_skip, w_up, w_adj, w_back, w_pred,
    split, merge,
    pred, g_out, g_skip, g_up, g_mid,
    patch, gpatch, enc_s, pool_s, coarse_s, pre_s, gd_s, gt_s, gct_s, acc_s,
):
    first, last = edge[0] == 1, edge[1] == 1
    for ref in (enc_s, gd_s):
        ref[:, :, 0:LANES] = jnp.zeros(ref.shape[:2] + (LANES,), BF16)
        ref[:, :, LANES + CELLS :] = jnp.zeros(ref.shape[:2] + (LANES,), BF16)
    for ref in (pool_s, coarse_s):
        ref[:, 0:LANES] = jnp.zeros((ref.shape[0], LANES), BF16)
        ref[:, LANES + CELLS :] = jnp.zeros((ref.shape[0], LANES), BF16)
    coarse_s[0:192, :] = jnp.zeros((192, WIDE), BF16)
    coarse_s[7 * 192 : 8 * 192, :] = jnp.zeros((192, WIDE), BF16)
    g_out[...] = jnp.zeros(g_out.shape, F32)

    def put_inflow(line, value):
        parts = dot(value, split[...])
        block = [rows_to_lanes(parts, 0, 16, w * LANES) for w in range(4)]
        patch[row(line, 64, 64), :] = jnp.concatenate(block, axis=0).astype(BF16)

    def put_gp(line, value):
        parts = dot(value, split[:, LANES : 3 * LANES])
        block = [rows_to_lanes(parts, 0, 8, w * LANES) for w in range(2)]
        gpatch[row(line, 16, 16), :] = jnp.concatenate(block, axis=0).astype(BF16)

    def edges(i, c):
        put_inflow(i, before[i])
        put_inflow(i + 13, after[i])
        return c

    def middle(i, c):
        put_inflow(i + 5, inflow[i])
        put_gp(i + 1, gp[i][4:68])
        return c

    lax.fori_loop(0, 5, edges, 0)
    lax.fori_loop(0, 8, middle, 0)
    put_gp(0, before[5][4:68])
    put_gp(9, after[5][4:68])

    def encode(xe, c):
        outside = (first & (xe < 2)) | (last & (xe > 5))
        v = dot(w_in[...], patch[row(xe, 256, 128), :]) + bias[...]
        v = jnp.where(outside, 0.0, jnp.maximum(v, 0.0)).astype(BF16).astype(F32)
        total = v[0:32]
        for p in range(1, 8):
            total = total + v[p * 32 : p * 32 + 32]
        put_coarse(pool_s, xe, total * 0.125)
        for px in range(2):
            for py in range(2):
                at = (px * 2 + py) * 64
                put_fine(enc_s, py, 2 * xe + px, v[at : at + 32], v[at + 32 : at + 64])
        return c

    lax.fori_loop(0, 8, encode, 0)

    def middle_level(xk, c):
        pre = jnp.zeros((64, CELLS), F32)
        for dy in range(3):
            pre = pre + dot(
                w_mid[:, dy * 288 : dy * 288 + 288],
                pool_s[row(xk, 288, 96), dy * LANES : dy * LANES + CELLS],
            )
        pre_s[xk] = pre
        outside = (first & (xk < 1)) | (last & (xk > 4))
        put_coarse(coarse_s, xk + 1, jnp.where(outside, 0.0, pre * jax.nn.sigmoid(pre)))
        return c

    lax.fori_loop(0, 6, middle_level, 0)

    def decode_pre(xc, rows):
        v = jnp.zeros((rows[1] - rows[0], CELLS), F32)
        for yw, (par, start) in enumerate(WINDOW):
            v = v + dot(
                w_skip[rows[0] : rows[1], yw * 512 : yw * 512 + 512],
                enc_s[par, row(2 * xc + 3, 512, 128), start : start + CELLS],
            )
        for dy in range(3):
            v = v + dot(
                w_up[rows[0] : rows[1], dy * 576 : dy * 576 + 576],
                coarse_s[row(xc + 1, 576, 192), dy * LANES : dy * LANES + CELLS],
            )
        return v

    def put_grad(xc, pxs, grad):
        for i, px in enumerate(pxs):
            for py in range(2):
                at = (i * 2 + py) * 64
                put_fine(gd_s, py, 2 * xc + px + 1, grad[at : at + 32], grad[at + 32 : at + 64])

    def decode(xc, c):
        v = decode_pre(xc, (0, 256))
        sigma = jax.nn.sigmoid(v)
        dec = (v * sigma).astype(BF16)
        cot = gpatch[row(2 * xc + 1, 32, 16), :]
        grad = dot(w_back[...], cot) * (sigma * (1.0 + v * (1.0 - sigma)))
        out = dot(w_pred[...], dec)
        for px in range(2):
            halves = []
            for pz in range(2):
                at = (px * 2 + pz) * 8
                halves.append(
                    jnp.concatenate(
                        [out[at : at + 8, y * LANES : y * LANES + LANES] for y in range(YC)],
                        axis=0,
                    )
                )
            line = jnp.concatenate(halves, axis=1)
            high = line.astype(BF16)
            low = (line - high.astype(F32)).astype(BF16)
            pred[2 * xc + px] = dot(high, merge[...]) + dot(low, merge[...])
        full = lax.dot_general(cot, dec, (((1,), (1,)), ((), ())), preferred_element_type=F32)
        for i, (px, py, pz) in enumerate(PARITIES):
            at = (px * 4 + pz * 2 + py) * 4
            g_out[...] += full[at : at + 4, i * 32 : i * 32 + 32]
        put_grad(xc, (0, 1), grad)
        gt_s[row(xc, CELLS, CELLS), :] = grad.T.astype(BF16)
        return c

    def rim(xc, px, line):
        v = decode_pre(xc, (px * 128, px * 128 + 128))
        sigma = jax.nn.sigmoid(v)
        back = dot(
            w_back[px * 128 : px * 128 + 128, px * 16 : px * 16 + 16],
            gpatch[line * 16 : line * 16 + 16, :],
        )
        put_grad(xc, (px,), back * (sigma * (1.0 + v * (1.0 - sigma))))

    rim(-1, 1, 0)
    rim(4, 0, 9)
    lax.fori_loop(0, 4, decode, 0)

    def coarse_grad(xc, c):
        v = jnp.zeros((64, CELLS), F32)
        for yw, (par, start) in enumerate(WINDOW):
            v = v + dot(
                w_adj[:, yw * 512 : yw * 512 + 512],
                gd_s[par, row(xc, 512, 256), start : start + CELLS],
            )
        pre = pre_s[xc + 1]
        sigma = jax.nn.sigmoid(pre)
        v = v * (sigma * (1.0 + pre * (1.0 - sigma)))
        gct_s[row(xc, CELLS, CELLS), :] = v.T.astype(BF16)
        return c

    lax.fori_loop(0, 4, coarse_grad, 0)

    for dy in range(3):
        total = jnp.zeros((288, 64), F32)
        for xc in range(4):
            total = total + dot(
                pool_s[(xc + 1) * 96 : (xc + 1) * 96 + 288, dy * LANES : dy * LANES + CELLS],
                gct_s[xc * CELLS : (xc + 1) * CELLS, :],
            )
        g_mid[dy] = total
    for yw, (par, start) in enumerate(WINDOW):
        total = jnp.zeros((512, 256), F32)
        for xc in range(4):
            total = total + dot(
                enc_s[par, (2 * xc + 3) * 128 : (2 * xc + 7) * 128, start : start + CELLS],
                gt_s[xc * CELLS : (xc + 1) * CELLS, :],
            )
        acc_s[yw * 512 : yw * 512 + 512, :] = total
    for a in range(3):
        for b in range(3):
            total = jnp.zeros((96, 32), F32)
            for i, (px, py, pz) in enumerate(PARITIES):
                at = (py + b) * 512 + (px + a) * 128 + pz * 32
                total = total + acc_s[at : at + 96, i * 32 : i * 32 + 32]
            g_skip[a, b] = total
    for dy in range(3):
        total = jnp.zeros((576, 256), F32)
        for xc in range(4):
            total = total + dot(
                coarse_s[(xc + 1) * 192 : (xc + 4) * 192, dy * LANES : dy * LANES + CELLS],
                gt_s[xc * CELLS : (xc + 1) * CELLS, :],
            )
        acc_s[dy * 576 : dy * 576 + 576, :] = total
    for a in range(3):
        for b in range(3):
            for e in range(3):
                total = jnp.zeros((64, 32), F32)
                for i, (px, py, pz) in enumerate(PARITIES):
                    dx, dy, dz = (px + a + 1) // 2, (py + b + 1) // 2, (pz + e + 1) // 2
                    at = dy * 576 + dx * 192 + dz * 64
                    total = total + acc_s[at : at + 64, i * 32 : i * 32 + 32]
                g_up[a, b, e] = total


def shards(inflow, speed_bin, bin_table, w_in, w_mid, w_dec, w_out, grad_pred):
    t_in, t_skip, t_up, t_adj, order, split, merge = (
        jnp.asarray(t, BF16) for t in place_tables()
    )
    lines = lambda f: jnp.pad(
        f.transpose(1, 2, 0, 3).reshape(f.shape[1], 64, 256), ((0, 0), (4, 4), (0, 0))
    )
    field, cot = lines(inflow), lines(grad_pred)
    devices = lax.axis_size("block")
    up = [(i, i + 1) for i in range(devices - 1)]
    down = [(i + 1, i) for i in range(devices - 1)]
    before = lax.ppermute(jnp.concatenate([field[3:8], cot[7:8]], axis=0), "block", up)
    after = lax.ppermute(jnp.concatenate([field[0:5], cot[0:1]], axis=0), "block", down)
    me = lax.axis_index("block")
    edge = jnp.stack([me == 0, me == devices - 1]).astype(jnp.int32)
    bias = jnp.tile(lax.dynamic_index_in_dim(bin_table, speed_bin[0], 0, False), 8)
    bias = bias.astype(F32)[:, None]
    spread = lambda t, w: (
        jnp.einsum("PkD,koc->PoDc", t, w.reshape((27,) + w.shape[3:]), preferred_element_type=F32)
        .astype(BF16)
        .reshape(256, -1)
    )
    k_in = spread(t_in, w_in)
    k_skip = spread(t_skip, w_dec[..., 64:])
    k_up = spread(t_up, w_dec[..., :64])
    k_mid = w_mid.transpose(3, 1, 0, 2, 4).reshape(64, 864)
    k_adj = (
        jnp.einsum(
            "kD,koc->cDo", t_adj, w_dec[..., :64].reshape(27, 32, 64), preferred_element_type=F32
        )
        .astype(BF16)
        .reshape(64, 2048)
    )
    k_back = (order[:, None, :, None] * w_out.T[None, :, None, :]).reshape(256, 32)
    k_pred = k_back.T
    vmem = pl.BlockSpec(memory_space=pltpu.VMEM)
    shape = jax.ShapeDtypeStruct
    pred, g_out, g_skip, g_up, g_mid = pl.pallas_call(
        body,
        out_shape=(
            shape((8, 64, 256), F32),
            shape((4, 32), F32),
            shape((3, 3, 96, 32), F32),
            shape((3, 3, 3, 64, 32), F32),
            shape((3, 288, 64), F32),
        ),
        in_specs=[pl.BlockSpec(memory_space=pltpu.SMEM)] + [vmem] * 14,
        out_specs=[vmem] * 5,
        scratch_shapes=[
            pltpu.VMEM((18 * 64, CELLS), BF16),
            pltpu.VMEM((10 * 16, CELLS), BF16),
            pltpu.VMEM((2, 16 * 128, WIDE), BF16),
            pltpu.VMEM((8 * 96, WIDE), BF16),
            pltpu.VMEM((8 * 192, WIDE), BF16),
            pltpu.VMEM((6, 64, CELLS), F32),
            pltpu.VMEM((2, 10 * 128, WIDE), BF16),
            pltpu.VMEM((4 * CELLS, 256), BF16),
            pltpu.VMEM((4 * CELLS, 64), BF16),
            pltpu.VMEM((2048, 256), F32),
        ],
        compiler_params=pltpu.CompilerParams(vmem_limit_bytes=56 * 1024 * 1024),
    )(
        edge, before, field, after, cot, bias, k_in, k_mid, k_skip, k_up, k_adj, k_back, k_pred,
        split, merge,
    )
    flat = jnp.concatenate(
        [g_skip.reshape(-1), g_up.reshape(-1), g_mid.reshape(-1), g_out.reshape(-1)]
    ).reshape(-1, 128)
    flat = lax.psum(flat, "block").reshape(-1)
    ends = np.cumsum([27648, 55296, 55296, 128])
    s_skip, s_up, s_mid, s_out = (
        flat[e - n : e] for e, n in zip(ends, (27648, 55296, 55296, 128))
    )
    grad_w_dec = jnp.concatenate(
        [s_up.reshape(3, 3, 3, 64, 32), s_skip.reshape(3, 3, 3, 32, 32)], axis=3
    ).swapaxes(3, 4)
    grad_w_mid = s_mid.reshape(3, 3, 3, 32, 64).transpose(1, 0, 2, 4, 3)
    pred = pred.reshape(8, 16, 4, 256).transpose(2, 0, 1, 3)
    return (pred, s_out.reshape(4, 32), grad_w_dec, grad_w_mid)


def solution(mesh):
    return jax.shard_map(
        shards,
        mesh=mesh,
        in_specs=(
            P(None, ("groups", "block"), None, None),
            P("groups"),
            P(),
            P(),
            P(),
            P(),
            P(),
            P(None, ("groups", "block"), None, None),
        ),
        out_specs=(
            P(None, ("groups", "block"), None, None),
            P("groups", None),
            P("groups", None, None, None, None),
            P("groups", None, None, None, None),
        ),
        check_vma=False,
    )
```

```python
import jax
import jax.numpy as jnp
import numpy as np
from jax import lax
from jax.experimental import pallas as pl
from jax.experimental.pallas import tpu as pltpu
from jax.sharding import PartitionSpec as P

F32, BF16 = jnp.float32, jnp.bfloat16
LANES = 128
YC = 8
CELLS = YC * LANES
WIDE = CELLS + 2 * LANES
WINDOW = ((1, 0), (0, LANES), (1, LANES), (0, 2 * LANES))
PARITIES = tuple((p // 4, p // 2 % 2, p % 2) for p in range(8))


def place_tables():
    fine = np.zeros((2, 3, 4), np.float32)
    for p in range(2):
        for a in range(3):
            fine[p, a, p + a] = 1
    t_in = np.einsum("pax,qby,rez->pqrabexzy", fine, fine, fine).reshape(8, 27, 64)
    t_in = np.einsum("PkD,cd->PkcDd", t_in, np.eye(4, dtype=np.float32)).reshape(8, 108, 256)
    order = np.zeros((8, 8), np.float32)
    for i, (px, py, pz) in enumerate(PARITIES):
        order[i, px * 4 + pz * 2 + py] = 1
    split = np.zeros((256, 512), np.float32)
    merge = np.zeros((256, 256), np.float32)
    for z in range(LANES):
        for w in range(4):
            if 0 <= 2 * z - 1 + w < 256:
                split[2 * z - 1 + w, w * LANES + z] = 1
        for p in range(2):
            merge[p * LANES + z, 2 * z + p] = 1
    take = np.zeros((80, 64), np.float32)
    give = np.zeros((64, 64), np.float32)
    for y in range(16):
        for c in range(4):
            take[4 + y * 4 + c, c * 16 + y] = 1
            give[c * 16 + y, y * 4 + c] = 1
    return t_in, order, split, merge, take, give


def dot(a, b):
    return jnp.dot(a, b, preferred_element_type=F32)


def shifted(v, by):
    z = lax.broadcasted_iota(jnp.int32, v.shape, 1) % LANES
    if by == 1:
        return jnp.where(z == 0, 0.0, pltpu.roll(v, 1, 1))
    return jnp.where(z == LANES - 1, 0.0, pltpu.roll(v, v.shape[1] - 1, 1))


def row(start, size, unit):
    return pl.ds(pl.multiple_of(start * unit, unit), size)


def put_fine(ref, par, line, low, high):
    block = jnp.concatenate([shifted(high, 1), low, high, shifted(low, -1)], axis=0)
    ref[par, row(line, 128, 128), LANES : LANES + CELLS] = block.astype(BF16)


def put_coarse(ref, plane, v):
    block = jnp.concatenate([shifted(v, 1), v, shifted(v, -1)], axis=0)
    n = 3 * v.shape[0]
    ref[row(plane, n, n), LANES : LANES + CELLS] = block.astype(BF16)


def rows_to_lanes(v, first, count, lane):
    return jnp.concatenate(
        [v[8 * y + first : 8 * y + first + count, lane : lane + LANES] for y in range(YC)], axis=1
    )


def body(
    edge, before, inflow, after, gp, bias, in_taps, w_mid, skip_taps, up_taps, adj_taps,
    w_back, w_pred, t_in, split, merge, take, give,
    pred, packed,
    patch, gpatch, enc_s, pool_s, coarse_s, pre_s, gd_s, gt_s, gct_s, acc_s,
    w_in, w_skip, w_up, w_adj, out_s, pack_s, mid_s, skip_s,
):
    build_kernels(in_taps, skip_taps, up_taps, adj_taps, t_in, w_in, w_skip, w_up, w_adj)
    first, last = edge[0] == 1, edge[1] == 1
    for ref in (enc_s, gd_s):
        ref[:, :, 0:LANES] = jnp.zeros(ref.shape[:2] + (LANES,), BF16)
        ref[:, :, LANES + CELLS :] = jnp.zeros(ref.shape[:2] + (LANES,), BF16)
    for ref in (pool_s, coarse_s):
        ref[:, 0:LANES] = jnp.zeros((ref.shape[0], LANES), BF16)
        ref[:, LANES + CELLS :] = jnp.zeros((ref.shape[0], LANES), BF16)
    coarse_s[0:192, :] = jnp.zeros((192, WIDE), BF16)
    coarse_s[7 * 192 : 8 * 192, :] = jnp.zeros((192, WIDE), BF16)
    out_s[...] = jnp.zeros(out_s.shape, F32)

    def fine_line(ref, i):
        rows = jnp.concatenate([ref[c, i] for c in range(4)], axis=0)
        return dot(take[...], rows).astype(BF16)

    def put_inflow(line, value):
        parts = dot(value, split[...])
        block = [rows_to_lanes(parts, 0, 16, w * LANES) for w in range(4)]
        patch[row(line, 64, 64), :] = jnp.concatenate(block, axis=0).astype(BF16)

    def put_gp(line, value):
        parts = dot(value, split[:, LANES : 3 * LANES])
        block = [rows_to_lanes(parts, 4, 8, w * LANES) for w in range(2)]
        gpatch[row(line, 16, 16), :] = jnp.concatenate(block, axis=0).astype(BF16)

    def edges(i, c):
        put_inflow(i, fine_line(before, i))
        put_inflow(i + 13, fine_line(after, i))
        return c

    def middle(i, c):
        put_inflow(i + 5, fine_line(inflow, i))
        put_gp(i + 1, fine_line(gp, i))
        return c

    lax.fori_loop(0, 5, edges, 0)
    lax.fori_loop(0, 8, middle, 0)
    put_gp(0, fine_line(before, 5))
    put_gp(9, fine_line(after, 5))

    def encode(xe, c):
        outside = (first & (xe < 2)) | (last & (xe > 5))
        v = dot(w_in[...], patch[row(xe, 256, 128), :]) + bias[...]
        v = jnp.where(outside, 0.0, jnp.maximum(v, 0.0)).astype(BF16).astype(F32)
        total = v[0:32]
        for p in range(1, 8):
            total = total + v[p * 32 : p * 32 + 32]
        put_coarse(pool_s, xe, total * 0.125)
        for px in range(2):
            for py in range(2):
                at = (px * 2 + py) * 64
                put_fine(enc_s, py, 2 * xe + px, v[at : at + 32], v[at + 32 : at + 64])
        return c

    lax.fori_loop(0, 8, encode, 0)

    def middle_level(xk, c):
        pre = jnp.zeros((64, CELLS), F32)
        for dy in range(3):
            pre = pre + dot(
                w_mid[:, dy * 288 : dy * 288 + 288],
                pool_s[row(xk, 288, 96), dy * LANES : dy * LANES + CELLS],
            )
        pre_s[xk] = pre
        outside = (first & (xk < 1)) | (last & (xk > 4))
        put_coarse(coarse_s, xk + 1, jnp.where(outside, 0.0, pre * jax.nn.sigmoid(pre)))
        return c

    lax.fori_loop(0, 6, middle_level, 0)

    def decode_pre(xc, rows):
        v = jnp.zeros((rows[1] - rows[0], CELLS), F32)
        for yw, (par, start) in enumerate(WINDOW):
            v = v + dot(
                w_skip[rows[0] : rows[1], yw * 512 : yw * 512 + 512],
                enc_s[par, row(2 * xc + 3, 512, 128), start : start + CELLS],
            )
        for dy in range(3):
            v = v + dot(
                w_up[rows[0] : rows[1], dy * 576 : dy * 576 + 576],
                coarse_s[row(xc + 1, 576, 192), dy * LANES : dy * LANES + CELLS],
            )
        return v

    def put_grad(xc, pxs, grad):
        for i, px in enumerate(pxs):
            for py in range(2):
                at = (i * 2 + py) * 64
                put_fine(gd_s, py, 2 * xc + px + 1, grad[at : at + 32], grad[at + 32 : at + 64])

    def decode(xc, c):
        v = decode_pre(xc, (0, 256))
        sigma = jax.nn.sigmoid(v)
        dec = (v * sigma).astype(BF16)
        cot = gpatch[row(2 * xc + 1, 32, 16), :]
        grad = dot(w_back[...], cot) * (sigma * (1.0 + v * (1.0 - sigma)))
        out = dot(w_pred[...], dec)
        for px in range(2):
            halves = []
            for pz in range(2):
                at = (px * 2 + pz) * 8
                halves.append(
                    jnp.concatenate(
                        [out[at : at + 8, y * LANES : y * LANES + LANES] for y in range(YC)],
                        axis=0,
                    )
                )
            line = jnp.concatenate(halves, axis=1)
            high = line.astype(BF16)
            low = (line - high.astype(F32)).astype(BF16)
            high = dot(give[...], high).astype(BF16)
            low = dot(give[...], low).astype(BF16)
            line = dot(high, merge[...]) + dot(low, merge[...])
            for o in range(4):
                pred[o, 2 * xc + px] = line[o * 16 : o * 16 + 16]
        full = lax.dot_general(cot, dec, (((1,), (1,)), ((), ())), preferred_element_type=F32)
        for i, (px, py, pz) in enumerate(PARITIES):
            at = (px * 4 + pz * 2 + py) * 4
            out_s[0:4, 0:32] += full[at : at + 4, i * 32 : i * 32 + 32]
        put_grad(xc, (0, 1), grad)
        gt_s[row(xc, CELLS, CELLS), :] = grad.T.astype(BF16)
        return c

    def rim(xc, px, line):
        v = decode_pre(xc, (px * 128, px * 128 + 128))
        sigma = jax.nn.sigmoid(v)
        back = dot(
            w_back[px * 128 : px * 128 + 128, px * 16 : px * 16 + 16],
            gpatch[line * 16 : line * 16 + 16, :],
        )
        put_grad(xc, (px,), back * (sigma * (1.0 + v * (1.0 - sigma))))

    rim(-1, 1, 0)
    rim(4, 0, 9)
    lax.fori_loop(0, 4, decode, 0)

    def coarse_grad(xc, c):
        v = jnp.zeros((64, CELLS), F32)
        for yw, (par, start) in enumerate(WINDOW):
            v = v + dot(
                w_adj[:, yw * 512 : yw * 512 + 512],
                gd_s[par, row(xc, 512, 256), start : start + CELLS],
            )
        pre = pre_s[xc + 1]
        sigma = jax.nn.sigmoid(pre)
        v = v * (sigma * (1.0 + pre * (1.0 - sigma)))
        gct_s[row(xc, CELLS, CELLS), :] = v.T.astype(BF16)
        return c

    lax.fori_loop(0, 4, coarse_grad, 0)

    for dy in range(3):
        total = jnp.zeros((288, 64), F32)
        for xc in range(4):
            total = total + dot(
                pool_s[(xc + 1) * 96 : (xc + 1) * 96 + 288, dy * LANES : dy * LANES + CELLS],
                gct_s[xc * CELLS : (xc + 1) * CELLS, :],
            )
        mid_s[dy] = total
    for yw, (par, start) in enumerate(WINDOW):
        total = jnp.zeros((512, 256), F32)
        for xc in range(4):
            total = total + dot(
                enc_s[par, (2 * xc + 3) * 128 : (2 * xc + 7) * 128, start : start + CELLS],
                gt_s[xc * CELLS : (xc + 1) * CELLS, :],
            )
        acc_s[yw * 512 : yw * 512 + 512, :] = total
    for a in range(3):
        for b in range(3):
            total = jnp.zeros((96, 32), F32)
            for i, (px, py, pz) in enumerate(PARITIES):
                at = (py + b) * 512 + (px + a) * 128 + pz * 32
                total = total + acc_s[at : at + 96, i * 32 : i * 32 + 32]
            skip_s[a * 3 + b] = total
    for dy in range(3):
        total = jnp.zeros((576, 256), F32)
        for xc in range(4):
            total = total + dot(
                coarse_s[(xc + 1) * 192 : (xc + 4) * 192, dy * LANES : dy * LANES + CELLS],
                gt_s[xc * CELLS : (xc + 1) * CELLS, :],
            )
        acc_s[dy * 576 : dy * 576 + 576, :] = total
    zero = jnp.zeros((128, 32), F32)
    for a in range(3):
        for b in range(3):
            taps = []
            mid = mid_s[b, a * 96 : a * 96 + 96, :]
            for e in range(3):
                total = jnp.zeros((64, 32), F32)
                for i, (px, py, pz) in enumerate(PARITIES):
                    dx, dy, dz = (px + a + 1) // 2, (py + b + 1) // 2, (pz + e + 1) // 2
                    at = dy * 576 + dx * 192 + dz * 64
                    total = total + acc_s[at : at + 64, i * 32 : i * 32 + 32]
                own = slice(e * 32, e * 32 + 32)
                taps.append(jnp.concatenate([total, skip_s[a * 3 + b, own], mid[own, 0:32]], axis=0))
            main = jnp.concatenate(taps + [zero], axis=1).T
            rest = jnp.concatenate([mid[:, 32:64], zero[0:32]], axis=0)
            rest = jnp.concatenate([rest, zero, zero, zero], axis=1).T
            for e in range(3):
                at = ((a * 3 + b) * 3 + e) * 40
                pack_s[at : at + 32, :] = main[e * 32 : e * 32 + 32]
                own = slice(e * 32, e * 32 + 32)
                pack_s[at + 32 : at + 40, :] = jnp.concatenate(
                    [rest[g * 8 : g * 8 + 8, own] for g in range(4)], axis=1
                )
    pack_s[1080:1088, :] = out_s[...]
    if pack_s.shape[0] > 1088:
        pack_s[1088:, :] = jnp.zeros((pack_s.shape[0] - 1088, 128), F32)
    packed[...] = pack_s[...].astype(packed.dtype)


def build_kernels(in_taps, skip_taps, up_taps, adj_taps, t_in, w_in, w_skip, w_up, w_adj):
    gap = jnp.zeros((32, 64), F32)
    w_skip[...] = jnp.zeros(w_skip.shape, BF16)
    for i, (px, py, pz) in enumerate(PARITIES):
        rows = slice(i * 32, i * 32 + 32)
        w_in[rows, :] = dot(in_taps[...], t_in[i]).astype(BF16)
        for a in range(3):
            for b in range(3):
                v = skip_taps[a * 3 + b].astype(F32)
                v = jnp.concatenate([gap[:, 0:32], v] if pz else [v, gap[:, 0:32]], axis=1)
                at = (py + b) * 512 + (px + a) * 128
                w_skip[rows, at : at + 128] = v.astype(BF16)
        pieces = []
        for dy in range(3):
            for dx in range(3):
                v = jnp.zeros((32, 192), F32)
                for a in range(3):
                    for b in range(3):
                        if (px + a + 1) // 2 == dx and (py + b + 1) // 2 == dy:
                            v = v + up_taps[a * 3 + b].astype(F32)
                e0, e1, e2 = v[:, 0:64], v[:, 64:128], v[:, 128:192]
                pieces += [gap, e0 + e1, e2] if pz else [e0, e1 + e2, gap]
        w_up[rows, :] = jnp.concatenate(pieces, axis=1).astype(BF16)
    zero = jnp.zeros((64, 32), F32)
    along_z = []
    for k in range(9):
        v = adj_taps[k].astype(F32)
        along_z.append(jnp.concatenate([v, zero], axis=1) + jnp.concatenate([zero, v], axis=1))
    reach = ((2,), (1, 2), (0, 1), (0,))
    for yw in range(4):
        for xw in range(4):
            v = jnp.zeros((64, 128), F32)
            for b in reach[yw]:
                for a in reach[xw]:
                    v = v + along_z[a * 3 + b]
            at = yw * 512 + xw * 128
            w_adj[:, at : at + 128] = v.astype(BF16)


def sum_body(n, packed, g_dec, g_mid, g_out, got, total_s, whole, flat, send1, recv1, send2, recv2):
    me = lax.axis_index("block")
    chunk = packed.shape[0] // n
    barrier = pltpu.get_barrier_semaphore()

    def greet(k, c):
        pl.semaphore_signal(
            barrier, 1, device_id={"block": lax.rem(me + k, n)},
            device_id_type=pl.DeviceIdType.MESH,
        )
        return c

    lax.fori_loop(1, n, greet, 0)
    pl.semaphore_wait(barrier, n - 1)

    def scatter(k):
        to = lax.rem(me + k, n)
        return pltpu.make_async_remote_copy(
            src_ref=packed.at[pl.ds(pl.multiple_of(to * chunk, 16), chunk)],
            dst_ref=got.at[k],
            send_sem=send1.at[k],
            recv_sem=recv1.at[k],
            device_id={"block": to},
            device_id_type=pl.DeviceIdType.MESH,
        )

    def gather(k):
        return pltpu.make_async_remote_copy(
            src_ref=total_s,
            dst_ref=whole.at[k],
            send_sem=send2.at[k],
            recv_sem=recv2.at[k],
            device_id={"block": lax.rem(me + k, n)},
            device_id_type=pl.DeviceIdType.MESH,
        )

    def each(f):
        lax.fori_loop(1, n, lambda k, c: (f(k), c)[1], 0)

    each(lambda k: scatter(k).start())

    def add(k, total):
        scatter(k).wait_recv()
        return total + got[k].astype(F32)

    own = packed[pl.ds(pl.multiple_of(me * chunk, 16), chunk), :].astype(F32)
    total = lax.fori_loop(1, n, add, own).astype(BF16)
    total_s[...] = total
    each(lambda k: gather(k).start())
    flat[pl.ds(pl.multiple_of(me * chunk, 16), chunk), :] = total.astype(F32)

    def place(k, c):
        gather(k).wait_recv()
        at = lax.rem(me - k + n, n) * chunk
        flat[pl.ds(pl.multiple_of(at, 16), chunk), :] = whole[k].astype(F32)
        return c

    lax.fori_loop(1, n, place, 0)
    each(lambda k: scatter(k).wait_send())
    each(lambda k: gather(k).wait_send())

    def unpack(k, c):
        main = flat[pl.ds(pl.multiple_of(k * 40, 8), 32), :]
        rest = flat[pl.ds(pl.multiple_of(k * 40 + 32, 8), 8), :]
        g_dec[k] = main[:, 0:96]
        g_mid[k] = jnp.concatenate(
            [main[:, 96:128]] + [rest[:, g * 32 : g * 32 + 32] for g in range(4)], axis=0
        )
        return c

    lax.fori_loop(0, 27, unpack, 0)
    g_out[...] = flat[1080:1084, 0:32]


def shards(inflow, speed_bin, bin_table, w_in, w_mid, w_dec, w_out, grad_pred):
    t_in, order, split, merge, take, give = (jnp.asarray(t, BF16) for t in place_tables())
    devices = lax.axis_size("block")
    up = [(i, i + 1) for i in range(devices - 1)]
    down = [(i + 1, i) for i in range(devices - 1)]
    ends = jnp.concatenate([inflow[:, 3:8], grad_pred[:, 7:8]], axis=1)
    starts = jnp.concatenate([inflow[:, 0:5], grad_pred[:, 0:1]], axis=1)
    before = lax.ppermute(ends, "block", up)
    after = lax.ppermute(starts, "block", down)
    me = lax.axis_index("block")
    edge = jnp.stack([me == 0, me == devices - 1]).astype(jnp.int32)
    bias = jnp.tile(lax.dynamic_index_in_dim(bin_table, speed_bin[0], 0, False), 8)
    bias = bias.astype(F32)[:, None]
    w_up, w_skip = w_dec[..., :64], w_dec[..., 64:]
    in_taps = w_in.transpose(3, 0, 1, 2, 4).reshape(32, 108)
    skip_taps = w_skip.transpose(0, 1, 3, 2, 4).reshape(9, 32, 96)
    up_taps = w_up.transpose(0, 1, 3, 2, 4).reshape(9, 32, 192)
    adj_taps = w_up[:, :, ::-1].transpose(0, 1, 4, 2, 3).reshape(9, 64, 96)
    k_mid = w_mid.transpose(3, 1, 0, 2, 4).reshape(64, 864)
    chunk = -(-1088 // (16 * devices)) * 16
    k_back = (order[:, None, :, None] * w_out.T[None, :, None, :]).reshape(256, 32)
    k_pred = k_back.T
    vmem = pl.BlockSpec(memory_space=pltpu.VMEM)
    shape = jax.ShapeDtypeStruct
    pred, packed = pl.pallas_call(
        body,
        out_shape=(shape((4, 8, 16, 256), F32), shape((chunk * devices, 128), BF16)),
        in_specs=[pl.BlockSpec(memory_space=pltpu.SMEM)] + [vmem] * 17,
        out_specs=[vmem] * 2,
        scratch_shapes=[
            pltpu.VMEM((18 * 64, CELLS), BF16),
            pltpu.VMEM((10 * 16, CELLS), BF16),
            pltpu.VMEM((2, 16 * 128, WIDE), BF16),
            pltpu.VMEM((8 * 96, WIDE), BF16),
            pltpu.VMEM((8 * 192, WIDE), BF16),
            pltpu.VMEM((6, 64, CELLS), F32),
            pltpu.VMEM((2, 10 * 128, WIDE), BF16),
            pltpu.VMEM((4 * CELLS, 256), BF16),
            pltpu.VMEM((4 * CELLS, 64), BF16),
            pltpu.VMEM((2048, 256), F32),
            pltpu.VMEM((256, 256), BF16),
            pltpu.VMEM((256, 2048), BF16),
            pltpu.VMEM((256, 1728), BF16),
            pltpu.VMEM((64, 2048), BF16),
            pltpu.VMEM((8, 128), F32),
            pltpu.VMEM((chunk * devices, 128), F32),
            pltpu.VMEM((3, 288, 64), F32),
            pltpu.VMEM((9, 96, 32), F32),
        ],
        compiler_params=pltpu.CompilerParams(vmem_limit_bytes=56 * 1024 * 1024),
    )(
        edge, before, inflow, after, grad_pred, bias, in_taps, k_mid, skip_taps, up_taps, adj_taps,
        k_back, k_pred, t_in, split, merge, take, give,
    )
    g_dec, g_mid, g_out = pl.pallas_call(
        lambda *refs: sum_body(devices, *refs),
        out_shape=(shape((27, 32, 96), F32), shape((27, 64, 32), F32), shape((4, 32), F32)),
        in_specs=[vmem],
        out_specs=[vmem] * 3,
        scratch_shapes=[
            pltpu.VMEM((devices, chunk, 128), BF16),
            pltpu.VMEM((chunk, 128), BF16),
            pltpu.VMEM((devices, chunk, 128), BF16),
            pltpu.VMEM((chunk * devices, 128), F32),
        ]
        + [pltpu.SemaphoreType.DMA((devices,))] * 4,
        compiler_params=pltpu.CompilerParams(
            collective_id=0, has_side_effects=True, vmem_limit_bytes=32 * 1024 * 1024
        ),
    )(packed)
    return (pred, g_out, g_dec.reshape(3, 3, 3, 32, 96), g_mid.reshape(3, 3, 3, 64, 32))


def solution(mesh):
    return jax.shard_map(
        shards,
        mesh=mesh,
        in_specs=(
            P(None, ("groups", "block"), None, None),
            P("groups"),
            P(),
            P(),
            P(),
            P(),
            P(),
            P(None, ("groups", "block"), None, None),
        ),
        out_specs=(
            P(None, ("groups", "block"), None, None),
            P("groups", None),
            P("groups", None, None, None, None),
            P("groups", None, None, None, None),
        ),
        check_vma=False,
    )
```

```python
import jax
import jax.numpy as jnp
import numpy as np
from jax import lax
from jax.experimental import pallas as pl
from jax.experimental.pallas import tpu as pltpu
from jax.sharding import PartitionSpec as P

F32, BF16 = jnp.float32, jnp.bfloat16
LANES = 128
YC = 8
CELLS = YC * LANES
WIDE = CELLS + 2 * LANES
WINDOW = ((1, 0), (0, LANES), (1, LANES), (0, 2 * LANES))
PARITIES = tuple((p // 4, p // 2 % 2, p % 2) for p in range(8))


def place_tables():
    fine = np.zeros((2, 3, 4), np.float32)
    for p in range(2):
        for a in range(3):
            fine[p, a, p + a] = 1
    t_in = np.einsum("pax,qby,rez->pqrabexzy", fine, fine, fine).reshape(8, 27, 64)
    t_in = np.einsum("PkD,cd->PkcDd", t_in, np.eye(4, dtype=np.float32)).reshape(8, 108, 256)
    order = np.zeros((8, 8), np.float32)
    for i, (px, py, pz) in enumerate(PARITIES):
        order[i, px * 4 + pz * 2 + py] = 1
    split = np.zeros((256, 512), np.float32)
    merge = np.zeros((256, 256), np.float32)
    for z in range(LANES):
        for w in range(4):
            if 0 <= 2 * z - 1 + w < 256:
                split[2 * z - 1 + w, w * LANES + z] = 1
        for p in range(2):
            merge[p * LANES + z, 2 * z + p] = 1
    take = np.zeros((80, 64), np.float32)
    give = np.zeros((64, 64), np.float32)
    for y in range(16):
        for c in range(4):
            take[4 + y * 4 + c, c * 16 + y] = 1
            give[c * 16 + y, y * 4 + c] = 1
    return t_in, order, split, merge, take, give


def sigmoid(v):
    return 0.5 * jnp.tanh(0.5 * v) + 0.5


def dot(a, b):
    return jnp.dot(a, b, preferred_element_type=F32)


def shifted(v, by):
    z = lax.broadcasted_iota(jnp.int32, v.shape, 1) % LANES
    if by == 1:
        return jnp.where(z == 0, 0.0, pltpu.roll(v, 1, 1))
    return jnp.where(z == LANES - 1, 0.0, pltpu.roll(v, v.shape[1] - 1, 1))


def row(start, size, unit):
    return pl.ds(pl.multiple_of(start * unit, unit), size)


def put_fine(ref, par, line, low, high):
    block = jnp.concatenate([shifted(high, 1), low, high, shifted(low, -1)], axis=0)
    ref[par, row(line, 128, 128), LANES : LANES + CELLS] = block.astype(BF16)


def put_coarse(ref, plane, v):
    block = jnp.concatenate([shifted(v, 1), v, shifted(v, -1)], axis=0)
    n = 3 * v.shape[0]
    ref[row(plane, n, n), LANES : LANES + CELLS] = block.astype(BF16)


def rows_to_lanes(v, first, count, lane):
    return jnp.concatenate(
        [v[8 * y + first : 8 * y + first + count, lane : lane + LANES] for y in range(YC)], axis=1
    )


def body(
    edge, before, inflow, after, gp, bias, in_taps, w_mid, skip_taps, up_taps, adj_taps,
    w_back, w_pred, t_in, split, merge, take, give,
    pred, packed,
    patch, gpatch, enc_s, pool_s, coarse_s, pre_s, gd_s, gt_s, gct_s, acc_s,
    w_in, w_skip, w_up, w_adj, out_s, pack_s, mid_s, skip_s,
):
    build_kernels(in_taps, skip_taps, up_taps, adj_taps, t_in, w_in, w_skip, w_up, w_adj)
    first, last = edge[0] == 1, edge[1] == 1
    for ref in (enc_s, gd_s):
        ref[:, :, 0:LANES] = jnp.zeros(ref.shape[:2] + (LANES,), BF16)
        ref[:, :, LANES + CELLS :] = jnp.zeros(ref.shape[:2] + (LANES,), BF16)
    for ref in (pool_s, coarse_s):
        ref[:, 0:LANES] = jnp.zeros((ref.shape[0], LANES), BF16)
        ref[:, LANES + CELLS :] = jnp.zeros((ref.shape[0], LANES), BF16)
    coarse_s[0:192, :] = jnp.zeros((192, WIDE), BF16)
    coarse_s[7 * 192 : 8 * 192, :] = jnp.zeros((192, WIDE), BF16)
    out_s[...] = jnp.zeros(out_s.shape, F32)

    def fine_line(ref, i):
        rows = jnp.concatenate([ref[c, i] for c in range(4)], axis=0)
        return dot(take[...], rows).astype(BF16)

    def put_inflow(line, value):
        parts = dot(value, split[...])
        block = [rows_to_lanes(parts, 0, 16, w * LANES) for w in range(4)]
        patch[row(line, 64, 64), :] = jnp.concatenate(block, axis=0).astype(BF16)

    def put_gp(line, value):
        parts = dot(value, split[:, LANES : 3 * LANES])
        block = [rows_to_lanes(parts, 4, 8, w * LANES) for w in range(2)]
        gpatch[row(line, 16, 16), :] = jnp.concatenate(block, axis=0).astype(BF16)

    def edges(i, c):
        put_inflow(i, fine_line(before, i))
        put_inflow(i + 13, fine_line(after, i))
        return c

    def middle(i, c):
        put_inflow(i + 5, fine_line(inflow, i))
        put_gp(i + 1, fine_line(gp, i))
        return c

    lax.fori_loop(0, 5, edges, 0)
    lax.fori_loop(0, 8, middle, 0)
    put_gp(0, fine_line(before, 5))
    put_gp(9, fine_line(after, 5))

    def encode(xe, c):
        outside = (first & (xe < 2)) | (last & (xe > 5))
        v = dot(w_in[...], patch[row(xe, 256, 128), :]) + bias[...]
        v = jnp.where(outside, 0.0, jnp.maximum(v, 0.0)).astype(BF16).astype(F32)
        total = v[0:32]
        for p in range(1, 8):
            total = total + v[p * 32 : p * 32 + 32]
        put_coarse(pool_s, xe, total * 0.125)
        for px in range(2):
            for py in range(2):
                at = (px * 2 + py) * 64
                put_fine(enc_s, py, 2 * xe + px, v[at : at + 32], v[at + 32 : at + 64])
        return c

    lax.fori_loop(0, 8, encode, 0)

    def middle_level(xk, c):
        pre = jnp.zeros((64, CELLS), F32)
        for dy in range(3):
            pre = pre + dot(
                w_mid[:, dy * 288 : dy * 288 + 288],
                pool_s[row(xk, 288, 96), dy * LANES : dy * LANES + CELLS],
            )
        pre_s[xk] = pre
        outside = (first & (xk < 1)) | (last & (xk > 4))
        put_coarse(coarse_s, xk + 1, jnp.where(outside, 0.0, pre * sigmoid(pre)))
        return c

    lax.fori_loop(0, 6, middle_level, 0)

    def decode_pre(xc, rows):
        v = jnp.zeros((rows[1] - rows[0], CELLS), F32)
        for yw, (par, start) in enumerate(WINDOW):
            v = v + dot(
                w_skip[rows[0] : rows[1], yw * 512 : yw * 512 + 512],
                enc_s[par, row(2 * xc + 3, 512, 128), start : start + CELLS],
            )
        for dy in range(3):
            v = v + dot(
                w_up[rows[0] : rows[1], dy * 576 : dy * 576 + 576],
                coarse_s[row(xc + 1, 576, 192), dy * LANES : dy * LANES + CELLS],
            )
        return v

    def put_grad(xc, pxs, grad):
        for i, px in enumerate(pxs):
            for py in range(2):
                at = (i * 2 + py) * 64
                put_fine(gd_s, py, 2 * xc + px + 1, grad[at : at + 32], grad[at + 32 : at + 64])

    def decode(xc, c):
        v = decode_pre(xc, (0, 256))
        sigma = sigmoid(v)
        dec = (v * sigma).astype(BF16)
        cot = gpatch[row(2 * xc + 1, 32, 16), :]
        grad = dot(w_back[...], cot) * (sigma * (1.0 + v * (1.0 - sigma)))
        out = dot(w_pred[...], dec)
        for px in range(2):
            halves = []
            for pz in range(2):
                at = (px * 2 + pz) * 8
                halves.append(
                    jnp.concatenate(
                        [out[at : at + 8, y * LANES : y * LANES + LANES] for y in range(YC)],
                        axis=0,
                    )
                )
            line = jnp.concatenate(halves, axis=1)
            high = line.astype(BF16)
            low = (line - high.astype(F32)).astype(BF16)
            high = dot(give[...], high).astype(BF16)
            low = dot(give[...], low).astype(BF16)
            line = dot(high, merge[...]) + dot(low, merge[...])
            for o in range(4):
                pred[o, 2 * xc + px] = line[o * 16 : o * 16 + 16]
        full = lax.dot_general(cot, dec, (((1,), (1,)), ((), ())), preferred_element_type=F32)
        for i, (px, py, pz) in enumerate(PARITIES):
            at = (px * 4 + pz * 2 + py) * 4
            out_s[0:4, 0:32] += full[at : at + 4, i * 32 : i * 32 + 32]
        put_grad(xc, (0, 1), grad)
        gt_s[row(xc, CELLS, CELLS), :] = grad.T.astype(BF16)
        return c

    def rim(xc, px, line):
        v = decode_pre(xc, (px * 128, px * 128 + 128))
        sigma = sigmoid(v)
        back = dot(
            w_back[px * 128 : px * 128 + 128, px * 16 : px * 16 + 16],
            gpatch[line * 16 : line * 16 + 16, :],
        )
        put_grad(xc, (px,), back * (sigma * (1.0 + v * (1.0 - sigma))))

    rim(-1, 1, 0)
    rim(4, 0, 9)
    lax.fori_loop(0, 4, decode, 0)

    def coarse_grad(xc, c):
        v = jnp.zeros((64, CELLS), F32)
        for yw, (par, start) in enumerate(WINDOW):
            v = v + dot(
                w_adj[:, yw * 512 : yw * 512 + 512],
                gd_s[par, row(xc, 512, 256), start : start + CELLS],
            )
        pre = pre_s[xc + 1]
        sigma = sigmoid(pre)
        v = v * (sigma * (1.0 + pre * (1.0 - sigma)))
        gct_s[row(xc, CELLS, CELLS), :] = v.T.astype(BF16)
        return c

    lax.fori_loop(0, 4, coarse_grad, 0)

    for dy in range(3):
        total = jnp.zeros((288, 64), F32)
        for xc in range(4):
            total = total + dot(
                pool_s[(xc + 1) * 96 : (xc + 1) * 96 + 288, dy * LANES : dy * LANES + CELLS],
                gct_s[xc * CELLS : (xc + 1) * CELLS, :],
            )
        mid_s[dy] = total
    for yw, (par, start) in enumerate(WINDOW):
        total = jnp.zeros((512, 256), F32)
        for xc in range(4):
            total = total + dot(
                enc_s[par, (2 * xc + 3) * 128 : (2 * xc + 7) * 128, start : start + CELLS],
                gt_s[xc * CELLS : (xc + 1) * CELLS, :],
            )
        acc_s[yw * 512 : yw * 512 + 512, :] = total
    for a in range(3):
        for b in range(3):
            total = jnp.zeros((96, 32), F32)
            for i, (px, py, pz) in enumerate(PARITIES):
                at = (py + b) * 512 + (px + a) * 128 + pz * 32
                total = total + acc_s[at : at + 96, i * 32 : i * 32 + 32]
            skip_s[a * 3 + b] = total
    for dy in range(3):
        total = jnp.zeros((576, 256), F32)
        for xc in range(4):
            total = total + dot(
                coarse_s[(xc + 1) * 192 : (xc + 4) * 192, dy * LANES : dy * LANES + CELLS],
                gt_s[xc * CELLS : (xc + 1) * CELLS, :],
            )
        acc_s[dy * 576 : dy * 576 + 576, :] = total
    zero = jnp.zeros((128, 32), F32)
    for a in range(3):
        for b in range(3):
            taps = []
            mid = mid_s[b, a * 96 : a * 96 + 96, :]
            for e in range(3):
                total = jnp.zeros((64, 32), F32)
                for i, (px, py, pz) in enumerate(PARITIES):
                    dx, dy, dz = (px + a + 1) // 2, (py + b + 1) // 2, (pz + e + 1) // 2
                    at = dy * 576 + dx * 192 + dz * 64
                    total = total + acc_s[at : at + 64, i * 32 : i * 32 + 32]
                own = slice(e * 32, e * 32 + 32)
                taps.append(jnp.concatenate([total, skip_s[a * 3 + b, own], mid[own, 0:32]], axis=0))
            main = jnp.concatenate(taps + [zero], axis=1).T
            rest = jnp.concatenate([mid[:, 32:64], zero[0:32]], axis=0)
            rest = jnp.concatenate([rest, zero, zero, zero], axis=1).T
            for e in range(3):
                at = ((a * 3 + b) * 3 + e) * 40
                pack_s[at : at + 32, :] = main[e * 32 : e * 32 + 32]
                own = slice(e * 32, e * 32 + 32)
                pack_s[at + 32 : at + 40, :] = jnp.concatenate(
                    [rest[g * 8 : g * 8 + 8, own] for g in range(4)], axis=1
                )
    pack_s[1080:1088, :] = out_s[...]
    if pack_s.shape[0] > 1088:
        pack_s[1088:, :] = jnp.zeros((pack_s.shape[0] - 1088, 128), F32)
    packed[...] = pack_s[...].astype(packed.dtype)


def build_kernels(in_taps, skip_taps, up_taps, adj_taps, t_in, w_in, w_skip, w_up, w_adj):
    gap = jnp.zeros((32, 64), F32)
    w_skip[...] = jnp.zeros(w_skip.shape, BF16)
    for i, (px, py, pz) in enumerate(PARITIES):
        rows = slice(i * 32, i * 32 + 32)
        w_in[rows, :] = dot(in_taps[...], t_in[i]).astype(BF16)
        for a in range(3):
            for b in range(3):
                v = skip_taps[a * 3 + b].astype(F32)
                v = jnp.concatenate([gap[:, 0:32], v] if pz else [v, gap[:, 0:32]], axis=1)
                at = (py + b) * 512 + (px + a) * 128
                w_skip[rows, at : at + 128] = v.astype(BF16)
        pieces = []
        for dy in range(3):
            for dx in range(3):
                v = jnp.zeros((32, 192), F32)
                for a in range(3):
                    for b in range(3):
                        if (px + a + 1) // 2 == dx and (py + b + 1) // 2 == dy:
                            v = v + up_taps[a * 3 + b].astype(F32)
                e0, e1, e2 = v[:, 0:64], v[:, 64:128], v[:, 128:192]
                pieces += [gap, e0 + e1, e2] if pz else [e0, e1 + e2, gap]
        w_up[rows, :] = jnp.concatenate(pieces, axis=1).astype(BF16)
    zero = jnp.zeros((64, 32), F32)
    along_z = []
    for k in range(9):
        v = adj_taps[k].astype(F32)
        along_z.append(jnp.concatenate([v, zero], axis=1) + jnp.concatenate([zero, v], axis=1))
    reach = ((2,), (1, 2), (0, 1), (0,))
    for yw in range(4):
        for xw in range(4):
            v = jnp.zeros((64, 128), F32)
            for b in reach[yw]:
                for a in reach[xw]:
                    v = v + along_z[a * 3 + b]
            at = yw * 512 + xw * 128
            w_adj[:, at : at + 128] = v.astype(BF16)


def sum_body(n, packed, g_dec, g_mid, g_out, got, total_s, whole, flat, send1, recv1, send2, recv2):
    me = lax.axis_index("block")
    chunk = packed.shape[0] // n
    barrier = pltpu.get_barrier_semaphore()

    def greet(k, c):
        pl.semaphore_signal(
            barrier, 1, device_id={"block": lax.rem(me + k, n)},
            device_id_type=pl.DeviceIdType.MESH,
        )
        return c

    lax.fori_loop(1, n, greet, 0)
    pl.semaphore_wait(barrier, n - 1)

    def scatter(k):
        to = lax.rem(me + k, n)
        return pltpu.make_async_remote_copy(
            src_ref=packed.at[pl.ds(pl.multiple_of(to * chunk, 16), chunk)],
            dst_ref=got.at[k],
            send_sem=send1.at[k],
            recv_sem=recv1.at[k],
            device_id={"block": to},
            device_id_type=pl.DeviceIdType.MESH,
        )

    def gather(k):
        return pltpu.make_async_remote_copy(
            src_ref=total_s,
            dst_ref=whole.at[k],
            send_sem=send2.at[k],
            recv_sem=recv2.at[k],
            device_id={"block": lax.rem(me + k, n)},
            device_id_type=pl.DeviceIdType.MESH,
        )

    def each(f):
        lax.fori_loop(1, n, lambda k, c: (f(k), c)[1], 0)

    each(lambda k: scatter(k).start())

    def add(k, total):
        scatter(k).wait_recv()
        return total + got[k].astype(F32)

    own = packed[pl.ds(pl.multiple_of(me * chunk, 16), chunk), :].astype(F32)
    total = lax.fori_loop(1, n, add, own).astype(BF16)
    total_s[...] = total
    each(lambda k: gather(k).start())
    flat[pl.ds(pl.multiple_of(me * chunk, 16), chunk), :] = total.astype(F32)

    def place(k, c):
        gather(k).wait_recv()
        at = lax.rem(me - k + n, n) * chunk
        flat[pl.ds(pl.multiple_of(at, 16), chunk), :] = whole[k].astype(F32)
        return c

    lax.fori_loop(1, n, place, 0)
    each(lambda k: scatter(k).wait_send())
    each(lambda k: gather(k).wait_send())

    def unpack(k, c):
        main = flat[pl.ds(pl.multiple_of(k * 40, 8), 32), :]
        rest = flat[pl.ds(pl.multiple_of(k * 40 + 32, 8), 8), :]
        g_dec[k] = main[:, 0:96]
        g_mid[k] = jnp.concatenate(
            [main[:, 96:128]] + [rest[:, g * 32 : g * 32 + 32] for g in range(4)], axis=0
        )
        return c

    lax.fori_loop(0, 27, unpack, 0)
    g_out[...] = flat[1080:1084, 0:32]


def shards(inflow, speed_bin, bin_table, w_in, w_mid, w_dec, w_out, grad_pred):
    t_in, order, split, merge, take, give = (jnp.asarray(t, BF16) for t in place_tables())
    devices = lax.axis_size("block")
    up = [(i, i + 1) for i in range(devices - 1)]
    down = [(i + 1, i) for i in range(devices - 1)]
    ends = jnp.concatenate([inflow[:, 3:8], grad_pred[:, 7:8]], axis=1)
    starts = jnp.concatenate([inflow[:, 0:5], grad_pred[:, 0:1]], axis=1)
    before = lax.ppermute(ends, "block", up)
    after = lax.ppermute(starts, "block", down)
    me = lax.axis_index("block")
    edge = jnp.stack([me == 0, me == devices - 1]).astype(jnp.int32)
    bias = jnp.tile(lax.dynamic_index_in_dim(bin_table, speed_bin[0], 0, False), 8)
    bias = bias.astype(F32)[:, None]
    w_up, w_skip = w_dec[..., :64], w_dec[..., 64:]
    in_taps = w_in.transpose(3, 0, 1, 2, 4).reshape(32, 108)
    skip_taps = w_skip.transpose(0, 1, 3, 2, 4).reshape(9, 32, 96)
    up_taps = w_up.transpose(0, 1, 3, 2, 4).reshape(9, 32, 192)
    adj_taps = w_up[:, :, ::-1].transpose(0, 1, 4, 2, 3).reshape(9, 64, 96)
    k_mid = w_mid.transpose(3, 1, 0, 2, 4).reshape(64, 864)
    chunk = -(-1088 // (16 * devices)) * 16
    k_back = (order[:, None, :, None] * w_out.T[None, :, None, :]).reshape(256, 32)
    k_pred = k_back.T
    vmem = pl.BlockSpec(memory_space=pltpu.VMEM)
    shape = jax.ShapeDtypeStruct
    pred, packed = pl.pallas_call(
        body,
        out_shape=(shape((4, 8, 16, 256), F32), shape((chunk * devices, 128), BF16)),
        in_specs=[pl.BlockSpec(memory_space=pltpu.SMEM)] + [vmem] * 17,
        out_specs=[vmem] * 2,
        scratch_shapes=[
            pltpu.VMEM((18 * 64, CELLS), BF16),
            pltpu.VMEM((10 * 16, CELLS), BF16),
            pltpu.VMEM((2, 16 * 128, WIDE), BF16),
            pltpu.VMEM((8 * 96, WIDE), BF16),
            pltpu.VMEM((8 * 192, WIDE), BF16),
            pltpu.VMEM((6, 64, CELLS), F32),
            pltpu.VMEM((2, 10 * 128, WIDE), BF16),
            pltpu.VMEM((4 * CELLS, 256), BF16),
            pltpu.VMEM((4 * CELLS, 64), BF16),
            pltpu.VMEM((2048, 256), F32),
            pltpu.VMEM((256, 256), BF16),
            pltpu.VMEM((256, 2048), BF16),
            pltpu.VMEM((256, 1728), BF16),
            pltpu.VMEM((64, 2048), BF16),
            pltpu.VMEM((8, 128), F32),
            pltpu.VMEM((chunk * devices, 128), F32),
            pltpu.VMEM((3, 288, 64), F32),
            pltpu.VMEM((9, 96, 32), F32),
        ],
        compiler_params=pltpu.CompilerParams(vmem_limit_bytes=56 * 1024 * 1024),
    )(
        edge, before, inflow, after, grad_pred, bias, in_taps, k_mid, skip_taps, up_taps, adj_taps,
        k_back, k_pred, t_in, split, merge, take, give,
    )
    g_dec, g_mid, g_out = pl.pallas_call(
        lambda *refs: sum_body(devices, *refs),
        out_shape=(shape((27, 32, 96), F32), shape((27, 64, 32), F32), shape((4, 32), F32)),
        in_specs=[vmem],
        out_specs=[vmem] * 3,
        scratch_shapes=[
            pltpu.VMEM((devices, chunk, 128), BF16),
            pltpu.VMEM((chunk, 128), BF16),
            pltpu.VMEM((devices, chunk, 128), BF16),
            pltpu.VMEM((chunk * devices, 128), F32),
        ]
        + [pltpu.SemaphoreType.DMA((devices,))] * 4,
        compiler_params=pltpu.CompilerParams(
            collective_id=0, has_side_effects=True, vmem_limit_bytes=32 * 1024 * 1024
        ),
    )(packed)
    return (pred, g_out, g_dec.reshape(3, 3, 3, 32, 96), g_mid.reshape(3, 3, 3, 64, 32))


def solution(mesh):
    return jax.shard_map(
        shards,
        mesh=mesh,
        in_specs=(
            P(None, ("groups", "block"), None, None),
            P("groups"),
            P(),
            P(),
            P(),
            P(),
            P(),
            P(None, ("groups", "block"), None, None),
        ),
        out_specs=(
            P(None, ("groups", "block"), None, None),
            P("groups", None),
            P("groups", None, None, None, None),
            P("groups", None, None, None, None),
        ),
        check_vma=False,
    )
```
